512 devices in a mesh: batch: 128 (over y_lo, x, z), rep: 4 (over y_hi, core).
Axes of the slice: x: 4, y: 4 (y_hi: 2, y_lo: 2; y = y_hi * 2 + y_lo), z: 16, core: 2. Of those that a mesh axis runs over, the one named last changes fastest.
Arguments:
- queries: bfloat16 [65536, 4096], P(('batch', 'rep')), may hold values from -24 to 24
- passages: bfloat16 [768, 4096], P('batch'), may hold values from -6 to 6
- positives: int32 [65536], P(('batch', 'rep')), may hold values from 0 to 767
- negatives: int32 [65536, 7], P(('batch', 'rep')), may hold values from 0 to 767
Outputs:
- query_grad: float32 [65536, 4096], P(('batch', 'rep'))
- passage_grad: float32 [768, 4096], P('batch')
The draws below stay inside these ranges and needn't reach their ends.
All inputs are finite; a program needn't handle non-finite values.
Results may differ from the reference program's by a relative error of at most 0.0014.
Values may be sent and summed in bfloat16 or wider, within the bound.
No kernel may reach another device: no remote copies, remote signals or barrier semaphores. Data moves between devices by JAX's collectives and lax.ppermute only.
A program may use at most 64 MiB of HBM per device.

```python
import math
import jax
import jax.numpy as jnp
import numpy as np
from jax import lax

D = 4096
QDEV = 128
NEG = 7
NQ = 65536
NP = 768
N_REP = 4


def pool_base(key):
    return jnp.clip(jax.random.normal(key, (NP, D), jnp.float32), -6.0, 6.0)


def draw_passages(key, part):
    base = pool_base(key)
    return base.astype(jnp.bfloat16)


def draw_queries(key, part):
    key = jax.random.fold_in(key, 7)
    values = jax.random.normal(key, (NQ, D), jnp.float32)
    return jnp.clip(values, -6.0, 6.0).astype(jnp.bfloat16)


def place_ends(values, own_key, smallest, largest):
    place = [jax.random.randint(jax.random.fold_in(own_key, axis), (), 0, length) for axis, length in enumerate(values.shape)]
    longest = values.shape.index(max(values.shape))
    next_to = place[:longest] + [(place[longest] + 1) % values.shape[longest]] + place[longest + 1:]
    return values.at[tuple(place)].set(smallest).at[tuple(next_to)].set(largest)


def rank_bounds(count, skew):
    weights = [(1 << 20) // math.isqrt(rank ** skew) + 1 for rank in range(1, count + 1)]
    scale = 1 + sum(weights) // (1 << 30)
    return np.cumsum(np.array([max(1, weight // scale) for weight in weights]))


def ranked(key, dims, count, lean):
    grid = rank_bounds(count, lean)
    lot = jax.random.randint(jax.random.fold_in(key, 1), dims, 0, int(grid[count - 1]))
    grade = jnp.searchsorted(jnp.asarray(grid, jnp.int32), lot, side="right")
    return jax.random.permutation(jax.random.fold_in(key, 2), count)[grade].astype(jnp.int32)


def setup_inputs(seed: int = 0) -> dict:
    keys = jax.random.split(jax.random.key(seed), 5)
    queries = draw_queries(jax.random.fold_in(keys[4], 71), 0)
    passages = draw_passages(jax.random.fold_in(keys[4], 71), 0)
    positives = place_ends(jax.random.randint(keys[2], (NQ,), 0, NP), jax.random.fold_in(keys[2], 1), 0, NP - 1).astype(jnp.int32)
    negatives = place_ends(ranked(keys[3], (NQ, NEG), NP, 2), jax.random.fold_in(keys[3], 3), 0, NP - 1).astype(jnp.int32)
    return dict(queries=queries, passages=passages, positives=positives, negatives=negatives)


def block_terms(query_rows, positive_rows, negative_rows, passages):
    columns = jnp.arange(NP, dtype=jnp.int32)
    scores = jnp.dot(query_rows, passages.T, preferred_element_type=jnp.float32) * 0.0625
    hard = jnp.take_along_axis(scores, negative_rows, axis=1)
    top = jnp.max(scores, axis=1)
    total = jnp.sum(jnp.exp(scores - top[:, None]), axis=1) + jnp.sum(jnp.exp(hard - top[:, None]), axis=1)
    lse = top + jnp.log(total)
    picked = negative_rows[:, :, None] == columns[None, None, :]
    extra = jnp.sum(jnp.where(picked, jnp.exp(hard - lse[:, None])[:, :, None], jnp.float32(0.0)), axis=1)
    target = (positive_rows[:, None] == columns[None, :]).astype(jnp.float32)
    weights = (jnp.exp(scores - lse[:, None]) + extra - target).astype(jnp.bfloat16)
    query_part = jnp.dot(weights, passages, preferred_element_type=jnp.float32) * 0.0625
    passage_part = jnp.dot(weights.T, query_rows, preferred_element_type=jnp.float32) * 0.0625
    return query_part, passage_part


def reference(queries, passages, positives, negatives):
    width = QDEV * N_REP
    count = NQ // width
    query_blocks = queries.reshape(count, width, D)
    positive_blocks = positives.reshape(count, width)
    negative_blocks = negatives.reshape(count, width, NEG)

    def step(carry, items):
        query_part, passage_part = block_terms(items[0], items[1], items[2], passages)
        return carry + passage_part, query_part

    start = jnp.zeros((NP, D), jnp.float32)
    passage_grad, query_parts = lax.scan(step, start, (query_blocks, positive_blocks, negative_blocks))
    return query_parts.reshape(NQ, D), passage_grad
```

```python
import functools

import jax
import jax.numpy as jnp
from jax import lax
from jax.experimental import pallas as pl
from jax.experimental.pallas import tpu as pltpu
from jax.sharding import Mesh
from jax.sharding import PartitionSpec as P

D = 4096
HALF = 2048
SLICE = 512
QDEV = 128
NP = 768
ROWS = 96
SIDE = 384
Y = ("yl", "yh")
VMEM_LIMIT = 60 * 1024 * 1024
F32, BF16 = jnp.float32, jnp.bfloat16


def shift(count, by):
    return [(i, (i + by) % count) for i in range(count)]


def along_y(by):
    place = lambda y: 2 * (y % 2) + y // 2
    return [(place(y), place((y + by) % 4)) for y in range(4)]


def call(kernel, outs, *args, smem=0, scratch=(), flops=0):
    in_specs = [pl.BlockSpec(memory_space=pltpu.SMEM)] * smem
    in_specs += [pl.BlockSpec(memory_space=pltpu.VMEM)] * (len(args) - smem)
    size = sum(a.size * a.dtype.itemsize for a in args) + sum(o.size * o.dtype.itemsize for o in outs)
    return pl.pallas_call(
        kernel,
        out_shape=outs,
        in_specs=in_specs,
        out_specs=[pl.BlockSpec(memory_space=pltpu.VMEM)] * len(outs),
        scratch_shapes=list(scratch),
        compiler_params=pltpu.CompilerParams(vmem_limit_bytes=VMEM_LIMIT),
        cost_estimate=pl.CostEstimate(flops=flops, bytes_accessed=size, transcendentals=0),
    )(*args)


def score_kernel(side_ref, qo, qx, *refs):
    pieces, (so, sx, pool), q2 = refs[:8], refs[8:11], refs[11]
    q2[:QDEV] = qo[...]
    q2[QDEV:] = qx[...]
    side = side_ref[0]
    for t in range(2):
        base = (side if t == 0 else 1 - side) * SIDE
        for s in range(4):
            pool[pl.ds(pl.multiple_of(base + ROWS * s, 32), ROWS), :] = pieces[4 * t + s][...]
    for n in range(3):
        cols = slice(256 * n, 256 * n + 256)
        part = lax.dot_general(q2[...], pool[cols, :], (((1,), (1,)), ((), ())), preferred_element_type=F32)
        so[:, cols] = part[:QDEV]
        sx[:, cols] = part[QDEV:]


def loss_kernel(so, sr, ids, pos, neg, w):
    scores = (so[...] + sr[...]) * 0.0625
    column = ids[...]
    count = jnp.ones(scores.shape, F32)
    for k in range(7):
        count += jnp.where(neg[:, k : k + 1] == column, 1.0, 0.0)
    top = jnp.max(scores, axis=1, keepdims=True)
    mass = jnp.exp(scores - top) * count
    total = jnp.sum(mass, axis=1, keepdims=True)
    w[...] = (mass / total - jnp.where(pos[...] == column, 1.0, 0.0)).astype(BF16)


def query_kernel(wo, wx, pool, go, gx, w2):
    w2[:QDEV] = wo[...]
    w2[QDEV:] = wx[...]
    for n in range(HALF // 512):
        cols = slice(512 * n, 512 * n + 512)
        part = jnp.dot(w2[...], pool[:, cols], preferred_element_type=F32) * 0.0625
        go[:, cols] = part[:QDEV]
        gx[:, cols] = part[QDEV:]


def pool_kernel(*refs):
    ws, qs, outs, w_all, q_all = refs[:8], refs[8:12], refs[12:16], refs[16], refs[17]
    for i in range(8):
        w_all[QDEV * i : QDEV * (i + 1), :] = ws[i][...]
    for i in range(4):
        q_all[2 * QDEV * i : 2 * QDEV * (i + 1), :] = qs[i][...]
    for n in range(3):
        part = lax.dot_general(
            w_all[:, 256 * n : 256 * n + 256], q_all[...], (((0,), (0,)), ((), ())), preferred_element_type=F32
        ) * 0.0625
        for lo in range(256 * n, 256 * n + 256, 32):
            side, rest = divmod(lo, SIDE)
            s, row = divmod(rest, ROWS)
            outs[s][ROWS * side + row : ROWS * side + row + 32, :] = part[lo - 256 * n : lo - 256 * n + 32]


def sum_kernel(a, b, c, d, out):
    out[...] = (a[...] + b[...]) + (c[...] + d[...])


def shards(queries, passages, positives, negatives):
    core = lax.axis_index("c")
    x = lax.axis_index("x")
    yl = lax.axis_index("yl")
    y = 2 * lax.axis_index("yh") + yl
    other = lambda a: lax.ppermute(a, "c", shift(2, 1))

    q_own = lax.dynamic_slice(queries, (0, core * HALF), (QDEV, HALF))
    q_out = lax.dynamic_slice(queries, (0, (1 - core) * HALF), (QDEV, HALF))
    q_oth = other(q_out)

    mine = lax.dynamic_slice(passages, (0, core * HALF), (6, HALF)).reshape(6, 16, 128)
    block = lax.all_gather(mine, "z", axis=0, tiled=True).reshape(ROWS, HALF)
    near = [block] + [lax.ppermute(block, "x", shift(4, s)) for s in range(1, 4)]
    far = [lax.ppermute(b, Y, along_y(1 if s in (0, 3) else -1)) for s, b in enumerate(near)]

    chip_queries = []
    for s in range(4):
        at = ((y + s) % 4) * SLICE
        part = jnp.concatenate([lax.dynamic_slice(q, (0, at), (QDEV, SLICE)) for q in (q_own, q_oth)])
        chip_queries.append(part if s == 0 else lax.ppermute(part, Y, along_y(s)))

    sd = jax.ShapeDtypeStruct
    s_own, s_out, pool = call(
        score_kernel,
        [sd((QDEV, NP), F32), sd((QDEV, NP), F32), sd((NP, HALF), BF16)],
        yl.reshape(1), q_own, q_oth, *near, *far,
        smem=1, scratch=[pltpu.VMEM((2 * QDEV, HALF), BF16)], flops=2 * 256 * NP * HALF,
    )
    s_oth = other(s_out)

    col = jnp.arange(NP, dtype=jnp.int32)
    side, s, z, r = col // SIDE, (col // ROWS) % 4, (col // 6) % 16, col % 6
    ids = ((side * 4 + (x - s) % 4) * 16 + z) * 6 + r
    w = call(
        loss_kernel, [sd((QDEV, NP), BF16)],
        s_own, s_oth, ids.reshape(1, NP), positives.reshape(QDEV, 1), negatives,
    )[0]

    ws = [w] + [lax.ppermute(w, Y, along_y(s)) for s in range(1, 4)]
    wx = [other(a) for a in ws]
    blocks = call(
        pool_kernel, [sd((2 * ROWS, SLICE), F32)] * 4,
        *[a for pair in zip(ws, wx) for a in pair], *chip_queries,
        scratch=[pltpu.VMEM((1024, NP), BF16), pltpu.VMEM((1024, SLICE), BF16)], flops=2 * 1024 * NP * SLICE,
    )
    got = [blocks[0]] + [lax.ppermute(blocks[s], "x", shift(4, -s)) for s in range(1, 4)]

    g_own, g_out = call(
        query_kernel, [sd((QDEV, HALF), F32)] * 2, w, wx[0], pool,
        scratch=[pltpu.VMEM((2 * QDEV, NP), BF16)], flops=2 * 256 * NP * HALF,
    )
    g_oth = other(g_out)
    low = jnp.where(core == 0, g_own, g_oth)
    high = jnp.where(core == 0, g_oth, g_own)
    query_grad = jnp.concatenate([low, high], axis=1)

    mid = call(sum_kernel, [sd((2 * ROWS, SLICE), F32)], *got)[0]
    spread = lax.all_to_all(mid.reshape(2, 16, 6, 4, 128), "z", 1, 0, tiled=False)
    owned = jnp.sum(spread, axis=0)
    full = lax.all_gather(owned.reshape(2, 6, SLICE), Y + ("c",), axis=0, tiled=False)
    full = jnp.where(yl == 0, full[:, 0], full[:, 1])
    passage_grad = full.reshape(2, 2, 2, 6, SLICE).transpose(3, 2, 1, 0, 4).reshape(6, D)
    return query_grad, passage_grad


def solution(mesh):
    fine = Mesh(mesh.devices.reshape(2, 4, 16, 2, 2), ("yl", "x", "z", "yh", "c"))
    every, pooled = ("yl", "x", "z", "yh", "c"), ("yl", "x", "z")
    return jax.shard_map(
        shards,
        mesh=fine,
        in_specs=(P(every, None), P(pooled, None), P(every), P(every, None)),
        out_specs=(P(every, None), P(pooled, None)),
        check_vma=False,
    )
```

```python
import jax
import jax.numpy as jnp
from jax import lax
from jax.experimental import pallas as pl
from jax.experimental.pallas import tpu as pltpu
from jax.sharding import Mesh
from jax.sharding import PartitionSpec as P

D = 4096
HALF = 2048
SLICE = 512
QDEV = 128
NP = 768
ROWS = 96
SIDE = 384
Y = ("yl", "yh")
VMEM_LIMIT = 60 * 1024 * 1024
F32, BF16 = jnp.float32, jnp.bfloat16


def shift(count, by):
    return [(i, (i + by) % count) for i in range(count)]


def along_y(by):
    place = lambda y: 2 * (y % 2) + y // 2
    return [(place(y), place((y + by) % 4)) for y in range(4)]


def call(kernel, outs, *args, smem=0, after=0, scratch=(), flops=0):
    count = len(args)
    in_specs = [pl.BlockSpec(memory_space=pltpu.SMEM)] * smem
    in_specs += [pl.BlockSpec(memory_space=pltpu.VMEM)] * (count - smem - after)
    in_specs += [pl.BlockSpec(memory_space=pl.ANY)] * after
    body = kernel
    if after:
        body = lambda *refs: kernel(*refs[: count - after], *refs[count:])
    size = sum(a.size * a.dtype.itemsize for a in args) + sum(o.size * o.dtype.itemsize for o in outs)
    return pl.pallas_call(
        body,
        out_shape=outs,
        in_specs=in_specs,
        out_specs=[pl.BlockSpec(memory_space=pltpu.VMEM)] * len(outs),
        scratch_shapes=list(scratch),
        compiler_params=pltpu.CompilerParams(vmem_limit_bytes=VMEM_LIMIT),
        cost_estimate=pl.CostEstimate(flops=flops, bytes_accessed=size, transcendentals=0),
    )(*args)


def score_kernel(side_ref, qo, qx, *refs):
    pieces, (so, sx, pool), q2 = refs[:8], refs[8:11], refs[11]
    q2[:QDEV] = qo[...]
    q2[QDEV:] = qx[...]
    side = side_ref[0]
    for t in range(2):
        base = (side if t == 0 else 1 - side) * SIDE
        for s in range(4):
            pool[pl.ds(pl.multiple_of(base + ROWS * s, 32), ROWS), :] = pieces[4 * t + s][...]
    for n in range(3):
        cols = slice(256 * n, 256 * n + 256)
        part = lax.dot_general(q2[...], pool[cols, :], (((1,), (1,)), ((), ())), preferred_element_type=F32)
        so[:, cols] = part[:QDEV]
        sx[:, cols] = part[QDEV:]


def loss_kernel(so, sr, ids, pos, neg, w):
    scores = (so[...] + sr[...]) * 0.0625
    column = ids[...]
    count = jnp.ones(scores.shape, F32)
    for k in range(7):
        count += jnp.where(neg[:, k : k + 1] == column, 1.0, 0.0)
    top = jnp.max(scores, axis=1, keepdims=True)
    mass = jnp.exp(scores - top) * count
    total = jnp.sum(mass, axis=1, keepdims=True)
    rounded = (mass / total - jnp.where(pos[...] == column, 1.0, 0.0)).astype(BF16)
    for i in range(4):
        w[i] = rounded


def query_kernel(here_ref, wo, wx, pool, go, gx, w2):
    here = here_ref[0]
    w2[:QDEV] = wo[here]
    w2[QDEV:] = wx[here]
    for n in range(HALF // 512):
        cols = slice(512 * n, 512 * n + 512)
        part = jnp.dot(w2[...], pool[:, cols], preferred_element_type=F32) * 0.0625
        go[:, cols] = part[:QDEV]
        gx[:, cols] = part[QDEV:]


def pool_kernel(at_ref, w_own, w_oth, qs, out, w_all):
    core, x = at_ref[0], at_ref[1]
    for i in range(4):
        for own, w in ((core, w_own), (1 - core, w_oth)):
            w_all[pl.ds(pl.multiple_of((2 * i + own) * QDEV, QDEV), QDEV), :] = w[i]
    for n in range(3):
        part = lax.dot_general(
            w_all[:, 256 * n : 256 * n + 256], qs[...], (((0,), (0,)), ((), ())), preferred_element_type=F32
        ) * 0.0625
        for lo in range(256 * n, 256 * n + 256, 32):
            side, rest = divmod(lo, SIDE)
            s, row = divmod(rest, ROWS)
            at = (x + 4 - s) % 4
            out[at, ROWS * side + row : ROWS * side + row + 32, :] = part[lo - 256 * n : lo - 256 * n + 32]


def x_sum_kernel(parts, out):
    total = (parts[0] + parts[1]) + (parts[2] + parts[3])
    for z in range(16):
        for side in range(2):
            rows = total[ROWS * side + 6 * z : ROWS * side + 6 * z + 6]
            for j in range(4):
                at = (4 * side + j) * 6
                out[z, at : at + 6, :] = rows[:, 128 * j : 128 * j + 128]


def z_sum_kernel(parts, out):
    total = parts[0]
    for z in range(1, 16):
        total = total + parts[z]
    for i in range(8):
        side = i // 4
        out[i] = total[24 * side : 24 * side + 24]


def last_kernel(parts, out):
    for i in range(8):
        yl, yh, core = i // 4, (i // 2) % 2, i % 2
        for j in range(4):
            at = core * HALF + (2 * yh + yl) * SLICE + 128 * j
            out[:, at : at + 128] = parts[i, 6 * j : 6 * j + 6, :]


def shards(queries, passages, positives, negatives):
    core = lax.axis_index("c")
    x = lax.axis_index("x")
    yl = lax.axis_index("yl")
    other = lambda a: lax.ppermute(a, "c", shift(2, 1))
    swap = lambda a, axes: lax.all_to_all(a, axes, 0, 0, tiled=True)
    sd = jax.ShapeDtypeStruct

    mine = lax.dynamic_slice(passages, (0, core * HALF), (6, HALF)).reshape(6, 16, 128)
    block = swap(jnp.broadcast_to(mine[None], (16, 6, 16, 128)), "z").reshape(ROWS, HALF)
    near = [block] + [lax.ppermute(block, "x", shift(4, s)) for s in range(1, 4)]
    far = [lax.ppermute(b, Y, along_y(1 if s in (0, 3) else -1)) for s, b in enumerate(near)]

    q_own = lax.dynamic_slice(queries, (0, core * HALF), (QDEV, HALF))
    q_oth = other(lax.dynamic_slice(queries, (0, (1 - core) * HALF), (QDEV, HALF)))
    slices = queries.reshape(QDEV, 2, 2, 2, SLICE).transpose(3, 2, 1, 0, 4)
    group = swap(slices.reshape(8, QDEV, SLICE), Y + ("c",))

    s_own, s_out, pool = call(
        score_kernel,
        [sd((QDEV, NP), F32), sd((QDEV, NP), F32), sd((NP, HALF), BF16)],
        yl.reshape(1), q_own, q_oth, *near, *far, group,
        smem=1, after=1, scratch=[pltpu.VMEM((2 * QDEV, HALF), BF16)], flops=2 * 256 * NP * HALF,
    )
    s_oth = other(s_out)

    col = jnp.arange(NP, dtype=jnp.int32)
    side, s, z, r = col // SIDE, (col // ROWS) % 4, (col // 6) % 16, col % 6
    ids = ((side * 4 + (x - s) % 4) * 16 + z) * 6 + r
    w4 = call(
        loss_kernel, [sd((4, QDEV, NP), BF16)],
        s_own, s_oth, ids.reshape(1, NP), positives.reshape(QDEV, 1), negatives,
    )[0]
    w_own = swap(w4, Y)
    w_oth = other(w_own)
    blocks = call(
        pool_kernel, [sd((4, 2 * ROWS, SLICE), F32)],
        jnp.stack([core, x]), w_own, w_oth, group.reshape(8 * QDEV, SLICE),
        smem=1, scratch=[pltpu.VMEM((1024, NP), BF16)], flops=2 * 1024 * NP * SLICE,
    )[0]
    by_x = swap(blocks, "x")

    here = 2 * yl + lax.axis_index("yh")
    g_own, g_out = call(
        query_kernel, [sd((QDEV, HALF), F32)] * 2, here.reshape(1), w_own, w_oth, pool, blocks,
        smem=1, after=1, scratch=[pltpu.VMEM((2 * QDEV, NP), BF16)], flops=2 * 256 * NP * HALF,
    )
    g_oth = other(g_out)
    low = jnp.where(core == 0, g_own, g_oth)
    high = jnp.where(core == 0, g_oth, g_own)
    query_grad = jnp.concatenate([low, high], axis=1)

    by_z = swap(call(x_sum_kernel, [sd((16, 48, 128), F32)], by_x)[0], "z")
    by_y = swap(call(z_sum_kernel, [sd((8, 24, 128), F32)], by_z)[0], Y + ("c",))
    passage_grad = call(last_kernel, [sd((6, D), F32)], by_y)[0]
    return query_grad, passage_grad


def solution(mesh):
    fine = Mesh(mesh.devices.reshape(2, 4, 16, 2, 2), ("yl", "x", "z", "yh", "c"))
    every, pooled = ("yl", "x", "z", "yh", "c"), ("yl", "x", "z")
    return jax.shard_map(
        shards,
        mesh=fine,
        in_specs=(P(every, None), P(pooled, None), P(every), P(every, None)),
        out_specs=(P(every, None), P(pooled, None)),
        check_vma=False,
    )
```

```python
import jax
import jax.numpy as jnp
from jax import lax
from jax.experimental import pallas as pl
from jax.experimental.pallas import tpu as pltpu
from jax.sharding import Mesh
from jax.sharding import PartitionSpec as P

D = 4096
HALF = 2048
SLICE = 512
QDEV = 128
NP = 768
ROWS = 96
SIDE = 384
Y = ("yl", "yh")
MIB = 1024 * 1024
F32, BF16 = jnp.float32, jnp.bfloat16


def shift(count, by):
    return [(i, (i + by) % count) for i in range(count)]


def along_y(by):
    place = lambda y: 2 * (y % 2) + y // 2
    return [(place(y), place((y + by) % 4)) for y in range(4)]


def call(kernel, outs, *args, smem=0, after=0, limit=16, scratch=(), flops=0):
    count = len(args)
    in_specs = [pl.BlockSpec(memory_space=pltpu.SMEM)] * smem
    in_specs += [pl.BlockSpec(memory_space=pltpu.VMEM)] * (count - smem - after)
    in_specs += [pl.BlockSpec(memory_space=pl.ANY)] * after
    body = kernel
    if after:
        body = lambda *refs: kernel(*refs[: count - after], *refs[count:])
    size = sum(a.size * a.dtype.itemsize for a in args) + sum(o.size * o.dtype.itemsize for o in outs)
    return pl.pallas_call(
        body,
        out_shape=outs,
        in_specs=in_specs,
        out_specs=[pl.BlockSpec(memory_space=pltpu.VMEM)] * len(outs),
        scratch_shapes=list(scratch),
        compiler_params=pltpu.CompilerParams(vmem_limit_bytes=limit * MIB),
        cost_estimate=pl.CostEstimate(flops=flops, bytes_accessed=size, transcendentals=0),
    )(*args)


def prep_kernel(at_ref, queries, q_oth, q2, *parts):
    core, y = at_ref[0], at_ref[1]
    q2[:QDEV] = queries[:, pl.ds(pl.multiple_of(core * HALF, 128), HALF)]
    q2[QDEV:] = q_oth[...]
    for s, part in enumerate(parts):
        part[...] = q2[:, pl.ds(pl.multiple_of((y + s) % 4 * SLICE, 128), SLICE)]


def hold_kernel(block, out):
    out[...] = block[...]


def mask_kernel(ids, pos, neg, count, target):
    column = ids[...]
    total = jnp.ones(count.shape, F32)
    for k in range(7):
        total += jnp.where(neg[:, k : k + 1] == column, 1.0, 0.0)
    count[...] = total
    target[...] = jnp.where(pos[...] == column, 1.0, 0.0)


def near_kernel(q2, *refs):
    pieces, (part, pool) = refs[:4], refs[4:]
    for s in range(4):
        pool[ROWS * s : ROWS * s + ROWS, :] = pieces[s][...]
    part[...] = lax.dot_general(q2[...], pool[...], (((1,), (1,)), ((), ())), preferred_element_type=F32)


def far_kernel(side_ref, q2, near, *refs):
    pieces, (so, sx, pool) = refs[:4], refs[4:]
    for s in range(4):
        pool[ROWS * s : ROWS * s + ROWS, :] = pieces[s][...]
    far = lax.dot_general(q2[...], pool[...], (((1,), (1,)), ((), ())), preferred_element_type=F32)
    for side, part in ((side_ref[0], near[...]), (1 - side_ref[0], far)):
        cols = pl.ds(pl.multiple_of(side * SIDE, 128), SIDE)
        so[:, cols] = part[:QDEV]
        sx[:, cols] = part[QDEV:]


def loss_kernel(so, sr, count, target, w):
    scores = (so[...] + sr[...]) * 0.0625
    top = jnp.max(scores, axis=1, keepdims=True)
    mass = jnp.exp(scores - top) * count[...]
    total = jnp.sum(mass, axis=1, keepdims=True)
    rounded = (mass / total - target[...]).astype(BF16)
    for i in range(4):
        w[i] = rounded


def query_kernel(at_ref, wo, wx, near, far, go, gx, w2):
    here, side = at_ref[0], at_ref[1]
    w2[:QDEV] = wo[here]
    w2[QDEV:] = wx[here]
    w_near = w2[:, pl.ds(pl.multiple_of(side * SIDE, 128), SIDE)]
    w_far = w2[:, pl.ds(pl.multiple_of((1 - side) * SIDE, 128), SIDE)]
    for n in range(HALF // 512):
        cols = slice(512 * n, 512 * n + 512)
        part = jnp.dot(w_near, near[:, cols], preferred_element_type=F32)
        part = (part + jnp.dot(w_far, far[:, cols], preferred_element_type=F32)) * 0.0625
        go[:, cols] = part[:QDEV]
        gx[:, cols] = part[QDEV:]


def join_kernel(core_ref, go, gx, out):
    core = core_ref[0]
    out[:, pl.ds(pl.multiple_of(core * HALF, 128), HALF)] = go[...]
    out[:, pl.ds(pl.multiple_of((1 - core) * HALF, 128), HALF)] = gx[...]


def pool_kernel(at_ref, w_own, w_oth, q0, q1, q2, q3, out, w_all, q_all):
    x, y, core = at_ref[0], at_ref[1], at_ref[2]
    for s, q in enumerate((q0, q1, q2, q3)):
        src = (y + 4 - s) % 4
        at = 2 * (src % 2) + src // 2
        q_all[2 * QDEV * s : 2 * QDEV * s + 2 * QDEV, :] = q[...]
        w_all[2 * QDEV * s : 2 * QDEV * s + QDEV, :] = w_own[at]
        w_all[2 * QDEV * s + QDEV : 2 * QDEV * s + 2 * QDEV, :] = w_oth[at]
    for n in range(3):
        part = lax.dot_general(
            w_all[:, 256 * n : 256 * n + 256], q_all[...], (((0,), (0,)), ((), ())), preferred_element_type=F32
        ) * 0.0625
        for lo in range(256 * n, 256 * n + 256, 32):
            side, rest = divmod(lo, SIDE)
            s, row = divmod(rest, ROWS)
            at = (x + 4 - s) % 4
            out[at, ROWS * side + row : ROWS * side + row + 32, :] = part[lo - 256 * n : lo - 256 * n + 32]


def x_sum_kernel(parts, out):
    total = (parts[0] + parts[1]) + (parts[2] + parts[3])
    for z in range(16):
        for side in range(2):
            rows = total[ROWS * side + 6 * z : ROWS * side + 6 * z + 6]
            for j in range(4):
                at = (4 * side + j) * 6
                out[z, at : at + 6, :] = rows[:, 128 * j : 128 * j + 128]


def z_sum_kernel(parts, out):
    total = parts[0]
    for z in range(1, 16):
        total = total + parts[z]
    for i in range(8):
        side = i // 4
        out[i] = total[24 * side : 24 * side + 24]


def last_kernel(parts, out):
    for i in range(8):
        yl, yh, core = i // 4, (i // 2) % 2, i % 2
        for j in range(4):
            at = core * HALF + (2 * yh + yl) * SLICE + 128 * j
            out[:, at : at + 128] = parts[i, 6 * j : 6 * j + 6, :]


def shards(queries, passages, positives, negatives):
    core = lax.axis_index("c")
    x = lax.axis_index("x")
    yl = lax.axis_index("yl")
    other = lambda a: lax.ppermute(a, "c", shift(2, 1))
    swap = lambda a, axes: lax.all_to_all(a, axes, 0, 0, tiled=True)
    sd = jax.ShapeDtypeStruct

    y = 2 * lax.axis_index("yh") + yl
    mine = lax.dynamic_slice(passages, (0, core * HALF), (6, HALF)).reshape(6, 16, 128)
    block = swap(jnp.broadcast_to(mine[None], (16, 6, 16, 128)), "z").reshape(ROWS, HALF)

    q_oth = other(lax.dynamic_slice(queries, (0, (1 - core) * HALF), (QDEV, HALF)))
    q2, *parts = call(
        prep_kernel, [sd((2 * QDEV, HALF), BF16)] + [sd((2 * QDEV, SLICE), BF16)] * 4,
        jnp.stack([core, y]), queries, q_oth, smem=1,
    )
    group = [parts[0]] + [lax.ppermute(parts[s], Y, along_y(s)) for s in range(1, 4)]
    col = jnp.arange(NP, dtype=jnp.int32)
    side, s, z, r = col // SIDE, (col // ROWS) % 4, (col // 6) % 16, col % 6
    ids = ((side * 4 + (x - s) % 4) * 16 + z) * 6 + r
    count, target = call(
        mask_kernel, [sd((QDEV, NP), F32)] * 2, ids.reshape(1, NP), positives.reshape(QDEV, 1), negatives
    )

    block = call(hold_kernel, [sd((ROWS, HALF), BF16)], block, q2, *group, count, target, after=7)[0]
    near = [block, lax.ppermute(block, "x", shift(4, 1)), None, lax.ppermute(block, "x", shift(4, 3))]
    near[2] = lax.ppermute(near[1], "x", shift(4, 1))
    far = [lax.ppermute(b, Y, along_y(by)) for b, by in zip(near, (1, -1, -1, 1))]

    s_near, pool_near = call(
        near_kernel, [sd((2 * QDEV, SIDE), F32), sd((SIDE, HALF), BF16)], q2, *near, flops=256 * NP * HALF
    )
    s_own, s_out, pool_far = call(
        far_kernel,
        [sd((QDEV, NP), F32), sd((QDEV, NP), F32), sd((SIDE, HALF), BF16)],
        yl.reshape(1), q2, s_near, *far, smem=1, flops=256 * NP * HALF,
    )
    s_oth = other(s_out)

    w4 = call(loss_kernel, [sd((4, QDEV, NP), BF16)], s_own, s_oth, count, target)[0]
    w_own = swap(w4, Y)
    w_oth = other(w_own)
    blocks = call(
        pool_kernel, [sd((4, 2 * ROWS, SLICE), F32)],
        jnp.stack([x, y, core]), w_own, w_oth, *group, smem=1,
        scratch=[pltpu.VMEM((1024, NP), BF16), pltpu.VMEM((1024, SLICE), BF16)], flops=2 * 1024 * NP * SLICE,
    )[0]
    sums = call(x_sum_kernel, [sd((16, 48, 128), F32)], swap(blocks, "x"))[0]
    by_z = swap(sums, "z")

    here = 2 * yl + lax.axis_index("yh")
    g_own, g_out = call(
        query_kernel, [sd((QDEV, HALF), F32)] * 2,
        jnp.stack([here, yl]), w_own, w_oth, pool_near, pool_far, sums,
        smem=1, after=1, scratch=[pltpu.VMEM((2 * QDEV, NP), BF16)], flops=2 * 256 * NP * HALF,
    )
    query_grad = call(join_kernel, [sd((QDEV, D), F32)], core.reshape(1), g_own, other(g_out), smem=1)[0]

    by_y = swap(call(z_sum_kernel, [sd((8, 24, 128), F32)], by_z, query_grad, after=1)[0], Y + ("c",))
    passage_grad = call(last_kernel, [sd((6, D), F32)], by_y)[0]
    return query_grad, passage_grad


def solution(mesh):
    fine = Mesh(mesh.devices.reshape(2, 4, 16, 2, 2), ("yl", "x", "z", "yh", "c"))
    every, pooled = ("yl", "x", "z", "yh", "c"), ("yl", "x", "z")
    return jax.shard_map(
        shards,
        mesh=fine,
        in_specs=(P(every, None), P(pooled, None), P(every), P(every, None)),
        out_specs=(P(every, None), P(pooled, None)),
        check_vma=False,
    )
```

```python
import jax
import jax.numpy as jnp
from jax import lax
from jax.experimental import pallas as pl
from jax.experimental.pallas import tpu as pltpu
from jax.sharding import Mesh
from jax.sharding import PartitionSpec as P

D = 4096
HALF = 2048
SLICE = 512
QDEV = 128
NP = 768
ROWS = 96
SIDE = 384
Y = ("yl", "yh")
MIB = 1024 * 1024
F32, BF16 = jnp.float32, jnp.bfloat16


def shift(count, by):
    return [(i, (i + by) % count) for i in range(count)]


def along_y(by):
    place = lambda y: 2 * (y % 2) + y // 2
    return [(place(y), place((y + by) % 4)) for y in range(4)]


def call(kernel, outs, *args, smem=0, after=0, out_spaces=None, limit=16, scratch=(), flops=0):
    count = len(args)
    in_specs = [pl.BlockSpec(memory_space=pltpu.SMEM)] * smem
    in_specs += [pl.BlockSpec(memory_space=pltpu.VMEM)] * (count - smem - after)
    in_specs += [pl.BlockSpec(memory_space=pl.ANY)] * after
    body = kernel
    if after:
        body = lambda *refs: kernel(*refs[: count - after], *refs[count:])
    size = sum(a.size * a.dtype.itemsize for a in args) + sum(o.size * o.dtype.itemsize for o in outs)
    return pl.pallas_call(
        body,
        out_shape=outs,
        in_specs=in_specs,
        out_specs=[pl.BlockSpec(memory_space=space) for space in out_spaces or [pltpu.VMEM] * len(outs)],
        scratch_shapes=list(scratch),
        compiler_params=pltpu.CompilerParams(vmem_limit_bytes=limit * MIB),
        cost_estimate=pl.CostEstimate(flops=flops, bytes_accessed=size, transcendentals=0),
    )(*args)


def prep_kernel(at_ref, queries, q_oth, q2, *parts):
    core, y = at_ref[0], at_ref[1]
    q2[:QDEV] = queries[:, pl.ds(pl.multiple_of(core * HALF, 128), HALF)]
    q2[QDEV:] = q_oth[...]
    for s, part in enumerate(parts):
        part[...] = q2[:, pl.ds(pl.multiple_of((y + s) % 4 * SLICE, 128), SLICE)]


def hold_kernel(block, out):
    out[...] = block[...]


def mask_kernel(ids, pos, neg, count, target):
    column = ids[...]
    total = jnp.ones(count.shape, F32)
    for k in range(7):
        total += jnp.where(neg[:, k : k + 1] == column, 1.0, 0.0)
    count[...] = total
    target[...] = jnp.where(pos[...] == column, 1.0, 0.0)


def near_kernel(q2, *refs):
    pieces, (part, pool) = refs[:4], refs[4:]
    for s in range(4):
        pool[ROWS * s : ROWS * s + ROWS, :] = pieces[s][...]
    part[...] = lax.dot_general(q2[...], pool[...], (((1,), (1,)), ((), ())), preferred_element_type=F32)


def far_kernel(side_ref, q2, near, *refs):
    pieces, (so, sx, pool) = refs[:4], refs[4:]
    for s in range(4):
        pool[ROWS * s : ROWS * s + ROWS, :] = pieces[s][...]
    far = lax.dot_general(q2[...], pool[...], (((1,), (1,)), ((), ())), preferred_element_type=F32)
    for side, part in ((side_ref[0], near[...]), (1 - side_ref[0], far)):
        cols = pl.ds(pl.multiple_of(side * SIDE, 128), SIDE)
        so[:, cols] = part[:QDEV]
        sx[:, cols] = part[QDEV:]


def loss_kernel(so, sr, count, target, w):
    scores = (so[...] + sr[...]) * 0.0625
    top = jnp.max(scores, axis=1, keepdims=True)
    mass = jnp.exp(scores - top) * count[...]
    total = jnp.sum(mass, axis=1, keepdims=True)
    rounded = (mass / total - target[...]).astype(BF16)
    for i in range(4):
        w[i] = rounded


def query_kernel(at_ref, wo, wx, near, far, go, gx, w2):
    here, side = at_ref[0], at_ref[1]
    w2[:QDEV] = wo[here]
    w2[QDEV:] = wx[here]
    w_near = w2[:, pl.ds(pl.multiple_of(side * SIDE, 128), SIDE)]
    w_far = w2[:, pl.ds(pl.multiple_of((1 - side) * SIDE, 128), SIDE)]
    for n in range(HALF // 512):
        cols = slice(512 * n, 512 * n + 512)
        part = jnp.dot(w_near, near[:, cols], preferred_element_type=F32)
        part = (part + jnp.dot(w_far, far[:, cols], preferred_element_type=F32)) * 0.0625
        go[:, cols] = part[:QDEV]
        gx[:, cols] = part[QDEV:]


def join_kernel(core_ref, go, gx, out, token, done):
    core = core_ref[0]
    copies = []
    for i, (part, at) in enumerate(((go, core), (gx, 1 - core))):
        cols = pl.ds(pl.multiple_of(at * HALF, 128), HALF)
        copies.append(pltpu.make_async_copy(part, out.at[:, cols], done.at[i]))
        copies[i].start()
    token[...] = jnp.zeros(token.shape, F32)
    for copy in copies:
        copy.wait()


def pool_kernel(at_ref, w_own, w_oth, q0, q1, q2, q3, out, w_all, q_all):
    x, y, core = at_ref[0], at_ref[1], at_ref[2]
    for s, q in enumerate((q0, q1, q2, q3)):
        src = (y + 4 - s) % 4
        at = 2 * (src % 2) + src // 2
        q_all[2 * QDEV * s : 2 * QDEV * s + 2 * QDEV, :] = q[...]
        w_all[2 * QDEV * s : 2 * QDEV * s + QDEV, :] = w_own[at]
        w_all[2 * QDEV * s + QDEV : 2 * QDEV * s + 2 * QDEV, :] = w_oth[at]
    for n in range(3):
        part = lax.dot_general(
            w_all[:, 256 * n : 256 * n + 256], q_all[...], (((0,), (0,)), ((), ())), preferred_element_type=F32
        ) * 0.0625
        for lo in range(256 * n, 256 * n + 256, 32):
            side, rest = divmod(lo, SIDE)
            s, row = divmod(rest, ROWS)
            at = (x + 4 - s) % 4
            out[at, ROWS * side + row : ROWS * side + row + 32, :] = part[lo - 256 * n : lo - 256 * n + 32]


def x_sum_kernel(parts, out):
    total = (parts[0] + parts[1]) + (parts[2] + parts[3])
    for z in range(16):
        for side in range(2):
            rows = total[ROWS * side + 6 * z : ROWS * side + 6 * z + 6]
            for j in range(4):
                at = (4 * side + j) * 6
                out[z, at : at + 6, :] = rows[:, 128 * j : 128 * j + 128]


def z_sum_kernel(parts, out):
    total = parts[0]
    for z in range(1, 16):
        total = total + parts[z]
    for i in range(8):
        side = i // 4
        out[i] = total[24 * side : 24 * side + 24]


def last_kernel(parts, out):
    for i in range(8):
        yl, yh, core = i // 4, (i // 2) % 2, i % 2
        for j in range(4):
            at = core * HALF + (2 * yh + yl) * SLICE + 128 * j
            out[:, at : at + 128] = parts[i, 6 * j : 6 * j + 6, :]


def shards(queries, passages, positives, negatives):
    core = lax.axis_index("c")
    x = lax.axis_index("x")
    yl = lax.axis_index("yl")
    other = lambda a: lax.ppermute(a, "c", shift(2, 1))
    swap = lambda a, axes: lax.all_to_all(a, axes, 0, 0, tiled=True)
    sd = jax.ShapeDtypeStruct

    y = 2 * lax.axis_index("yh") + yl
    mine = lax.dynamic_slice(passages, (0, core * HALF), (6, HALF)).reshape(6, 16, 128)
    block = swap(jnp.broadcast_to(mine[None], (16, 6, 16, 128)), "z").reshape(ROWS, HALF)

    q_oth = other(lax.dynamic_slice(queries, (0, (1 - core) * HALF), (QDEV, HALF)))
    q2, *parts = call(
        prep_kernel, [sd((2 * QDEV, HALF), BF16)] + [sd((2 * QDEV, SLICE), BF16)] * 4,
        jnp.stack([core, y]), queries, q_oth, smem=1,
    )
    group = [parts[0]] + [lax.ppermute(parts[s], Y, along_y(s)) for s in range(1, 4)]
    col = jnp.arange(NP, dtype=jnp.int32)
    side, s, z, r = col // SIDE, (col // ROWS) % 4, (col // 6) % 16, col % 6
    ids = ((side * 4 + (x - s) % 4) * 16 + z) * 6 + r
    count, target = call(
        mask_kernel, [sd((QDEV, NP), F32)] * 2, ids.reshape(1, NP), positives.reshape(QDEV, 1), negatives
    )

    block = call(hold_kernel, [sd((ROWS, HALF), BF16)], block, q2, *group, count, target, after=7)[0]
    far0 = lax.ppermute(block, Y, along_y(1))
    near = [block] + [lax.ppermute(block, "x", shift(4, by)) for by in (1, 2, 3)]
    far = [
        far0,
        lax.ppermute(far0, "x", shift(4, 1)),
        lax.ppermute(near[2], Y, along_y(1)),
        lax.ppermute(far0, "x", shift(4, 3)),
    ]

    s_near, pool_near = call(
        near_kernel, [sd((2 * QDEV, SIDE), F32), sd((SIDE, HALF), BF16)], q2, *near, flops=256 * NP * HALF
    )
    s_own, s_out, pool_far = call(
        far_kernel,
        [sd((QDEV, NP), F32), sd((QDEV, NP), F32), sd((SIDE, HALF), BF16)],
        yl.reshape(1), q2, s_near, *far, smem=1, flops=256 * NP * HALF,
    )
    s_oth = other(s_out)

    w4 = call(loss_kernel, [sd((4, QDEV, NP), BF16)], s_own, s_oth, count, target)[0]
    w_own = swap(w4, Y)
    w_oth = other(w_own)
    blocks = call(
        pool_kernel, [sd((4, 2 * ROWS, SLICE), F32)],
        jnp.stack([x, y, core]), w_own, w_oth, *group, smem=1,
        scratch=[pltpu.VMEM((1024, NP), BF16), pltpu.VMEM((1024, SLICE), BF16)], flops=2 * 1024 * NP * SLICE,
    )[0]
    sums = call(x_sum_kernel, [sd((16, 48, 128), F32)], swap(blocks, "x"))[0]
    by_z = swap(sums, "z")

    here = 2 * yl + lax.axis_index("yh")
    g_own, g_out = call(
        query_kernel, [sd((QDEV, HALF), F32)] * 2,
        jnp.stack([here, yl]), w_own, w_oth, pool_near, pool_far, sums,
        smem=1, after=1, scratch=[pltpu.VMEM((2 * QDEV, NP), BF16)], flops=2 * 256 * NP * HALF,
    )
    query_grad, token = call(
        join_kernel, [sd((QDEV, D), F32), sd((8, 128), F32)], core.reshape(1), g_own, other(g_out),
        smem=1, out_spaces=(pltpu.HBM, pltpu.VMEM), scratch=[pltpu.SemaphoreType.DMA((2,))],
    )

    by_y = swap(call(z_sum_kernel, [sd((8, 24, 128), F32)], by_z, token, after=1)[0], Y + ("c",))
    passage_grad = call(last_kernel, [sd((6, D), F32)], by_y)[0]
    return query_grad, passage_grad


def solution(mesh):
    fine = Mesh(mesh.devices.reshape(2, 4, 16, 2, 2), ("yl", "x", "z", "yh", "c"))
    every, pooled = ("yl", "x", "z", "yh", "c"), ("yl", "x", "z")
    return jax.shard_map(
        shards,
        mesh=fine,
        in_specs=(P(every, None), P(pooled, None), P(every), P(every, None)),
        out_specs=(P(every, None), P(pooled, None)),
        check_vma=False,
    )
```

```python
import jax
import jax.numpy as jnp
from jax import lax
from jax.experimental import pallas as pl
from jax.experimental.pallas import tpu as pltpu
from jax.sharding import Mesh
from jax.sharding import PartitionSpec as P

D = 4096
HALF = 2048
SLICE = 512
QDEV = 128
NP = 768
ROWS = 96
SIDE = 384
Y = ("yl", "yh")
MIB = 1024 * 1024
F32, BF16 = jnp.float32, jnp.bfloat16


def shift(count, by):
    return [(i, (i + by) % count) for i in range(count)]


def along_y(by):
    place = lambda y: 2 * (y % 2) + y // 2
    return [(place(y), place((y + by) % 4)) for y in range(4)]


def call(kernel, outs, *args, smem=0, after=0, out_spaces=None, limit=16, scratch=(), flops=0):
    count = len(args)
    in_specs = [pl.BlockSpec(memory_space=pltpu.SMEM)] * smem
    in_specs += [pl.BlockSpec(memory_space=pltpu.VMEM)] * (count - smem - after)
    in_specs += [pl.BlockSpec(memory_space=pl.ANY)] * after
    body = kernel
    if after:
        body = lambda *refs: kernel(*refs[: count - after], *refs[count:])
    size = sum(a.size * a.dtype.itemsize for a in args) + sum(o.size * o.dtype.itemsize for o in outs)
    return pl.pallas_call(
        body,
        out_shape=outs,
        in_specs=in_specs,
        out_specs=[pl.BlockSpec(memory_space=space) for space in out_spaces or [pltpu.VMEM] * len(outs)],
        scratch_shapes=list(scratch),
        compiler_params=pltpu.CompilerParams(vmem_limit_bytes=limit * MIB),
        cost_estimate=pl.CostEstimate(flops=flops, bytes_accessed=size, transcendentals=0),
    )(*args)


def prep_kernel(at_ref, queries, q_oth, q2, *parts):
    core, y = at_ref[0], at_ref[1]
    q2[:QDEV] = queries[:, pl.ds(pl.multiple_of(core * HALF, 128), HALF)]
    q2[QDEV:] = q_oth[...]
    for s, part in enumerate(parts):
        part[...] = q2[:, pl.ds(pl.multiple_of((y + s) % 4 * SLICE, 128), SLICE)]


def hold_kernel(block, out):
    out[...] = block[...]


def mask_kernel(ids, pos, neg, count, target):
    column = ids[...]
    total = jnp.ones(count.shape, F32)
    for k in range(7):
        total += jnp.where(neg[:, k : k + 1] == column, 1.0, 0.0)
    count[...] = total
    target[...] = jnp.where(pos[...] == column, 1.0, 0.0)


def near_kernel(q2, *refs):
    pieces, (part, pool) = refs[:4], refs[4:]
    for s in range(4):
        pool[ROWS * s : ROWS * s + ROWS, :] = pieces[s][...]
    part[...] = lax.dot_general(q2[...], pool[...], (((1,), (1,)), ((), ())), preferred_element_type=F32)


def far_kernel(side_ref, q2, near, *refs):
    pieces, (so, sx, pool) = refs[:4], refs[4:]
    for s in range(4):
        pool[ROWS * s : ROWS * s + ROWS, :] = pieces[s][...]
    far = lax.dot_general(q2[...], pool[...], (((1,), (1,)), ((), ())), preferred_element_type=F32)
    for side, part in ((side_ref[0], near[...]), (1 - side_ref[0], far)):
        cols = pl.ds(pl.multiple_of(side * SIDE, 128), SIDE)
        so[:, cols] = part[:QDEV]
        sx[:, cols] = part[QDEV:]


def loss_kernel(so, sr, count, target, w):
    scores = (so[...] + sr[...]) * 0.0625
    top = jnp.max(scores, axis=1, keepdims=True)
    mass = jnp.exp(scores - top) * count[...]
    total = jnp.sum(mass, axis=1, keepdims=True)
    rounded = (mass / total - target[...]).astype(BF16)
    for i in range(4):
        w[i] = rounded


def query_kernel(at_ref, wo, wx, near, far, go, gx, w2):
    here, side = at_ref[0], at_ref[1]
    w2[:QDEV] = wo[here]
    w2[QDEV:] = wx[here]
    w_near = w2[:, pl.ds(pl.multiple_of(side * SIDE, 128), SIDE)]
    w_far = w2[:, pl.ds(pl.multiple_of((1 - side) * SIDE, 128), SIDE)]
    for n in range(HALF // 512):
        cols = slice(512 * n, 512 * n + 512)
        part = jnp.dot(w_near, near[:, cols], preferred_element_type=F32)
        part = (part + jnp.dot(w_far, far[:, cols], preferred_element_type=F32)) * 0.0625
        go[:, cols] = part[:QDEV]
        gx[:, cols] = part[QDEV:]


def join_kernel(core_ref, go, gx, out, token, done):
    core = core_ref[0]
    copies = []
    for i, (part, at) in enumerate(((go, core), (gx, 1 - core))):
        cols = pl.ds(pl.multiple_of(at * HALF, 128), HALF)
        copies.append(pltpu.make_async_copy(part, out.at[:, cols], done.at[i]))
        copies[i].start()
    token[...] = jnp.zeros(token.shape, F32)
    for copy in copies:
        copy.wait()


def pool_kernel(at_ref, w_own, w_oth, q0, q1, q2, q3, out, w_all, q_all):
    x, y, core = at_ref[0], at_ref[1], at_ref[2]
    for s, q in enumerate((q0, q1, q2, q3)):
        src = (y + 4 - s) % 4
        at = 2 * (src % 2) + src // 2
        q_all[2 * QDEV * s : 2 * QDEV * s + 2 * QDEV, :] = q[...]
        w_all[2 * QDEV * s : 2 * QDEV * s + QDEV, :] = w_own[at]
        w_all[2 * QDEV * s + QDEV : 2 * QDEV * s + 2 * QDEV, :] = w_oth[at]
    for n in range(3):
        part = lax.dot_general(
            w_all[:, 256 * n : 256 * n + 256], q_all[...], (((0,), (0,)), ((), ())), preferred_element_type=F32
        ) * 0.0625
        for lo in range(256 * n, 256 * n + 256, 32):
            side, rest = divmod(lo, SIDE)
            s, row = divmod(rest, ROWS)
            at = (x + 4 - s) % 4
            out[at, ROWS * side + row : ROWS * side + row + 32, :] = part[lo - 256 * n : lo - 256 * n + 32]


def x_sum_kernel(parts, out):
    total = (parts[0] + parts[1]) + (parts[2] + parts[3])
    for z in range(16):
        for side in range(2):
            rows = total[ROWS * side + 6 * z : ROWS * side + 6 * z + 6]
            for j in range(4):
                at = (4 * side + j) * 6
                out[z, at : at + 6, :] = rows[:, 128 * j : 128 * j + 128]


def z_sum_kernel(parts, out):
    total = parts[0]
    for z in range(1, 16):
        total = total + parts[z]
    for i in range(8):
        side = i // 4
        out[i] = total[24 * side : 24 * side + 24]


def last_kernel(parts, out):
    for i in range(8):
        yl, yh, core = i // 4, (i // 2) % 2, i % 2
        for j in range(4):
            at = core * HALF + (2 * yh + yl) * SLICE + 128 * j
            out[:, at : at + 128] = parts[i, 6 * j : 6 * j + 6, :]


def shards(queries, passages, positives, negatives):
    core = lax.axis_index("c")
    x = lax.axis_index("x")
    yl = lax.axis_index("yl")
    other = lambda a: lax.ppermute(a, "c", shift(2, 1))
    swap = lambda a, axes: lax.all_to_all(a, axes, 0, 0, tiled=True)
    sd = jax.ShapeDtypeStruct

    y = 2 * lax.axis_index("yh") + yl
    mine = lax.dynamic_slice(passages, (0, core * HALF), (6, HALF)).reshape(6, 16, 128)
    block = swap(jnp.broadcast_to(mine[None], (16, 6, 16, 128)), "z").reshape(ROWS, HALF)

    q_oth = other(lax.dynamic_slice(queries, (0, (1 - core) * HALF), (QDEV, HALF)))
    q2, *parts = call(
        prep_kernel, [sd((2 * QDEV, HALF), BF16)] + [sd((2 * QDEV, SLICE), BF16)] * 4,
        jnp.stack([core, y]), queries, q_oth, smem=1,
    )
    sent = {s: lax.ppermute(parts[s], Y, along_y(s)) for s in (2, 1, 3)}
    group = [parts[0]] + [sent[s] for s in (1, 2, 3)]
    col = jnp.arange(NP, dtype=jnp.int32)
    side, s, z, r = col // SIDE, (col // ROWS) % 4, (col // 6) % 16, col % 6
    ids = ((side * 4 + (x - s) % 4) * 16 + z) * 6 + r
    count, target = call(
        mask_kernel, [sd((QDEV, NP), F32)] * 2, ids.reshape(1, NP), positives.reshape(QDEV, 1), negatives
    )

    block = call(hold_kernel, [sd((ROWS, HALF), BF16)], block, q2, *group, count, target, after=7)[0]
    far0 = lax.ppermute(block, Y, along_y(1))
    near = [block] + [lax.ppermute(block, "x", shift(4, by)) for by in (1, 2, 3)]
    far = [
        far0,
        lax.ppermute(far0, "x", shift(4, 1)),
        lax.ppermute(near[2], Y, along_y(1)),
        lax.ppermute(far0, "x", shift(4, 3)),
    ]

    s_near, pool_near = call(
        near_kernel, [sd((2 * QDEV, SIDE), F32), sd((SIDE, HALF), BF16)], q2, *near, flops=256 * NP * HALF
    )
    s_own, s_out, pool_far = call(
        far_kernel,
        [sd((QDEV, NP), F32), sd((QDEV, NP), F32), sd((SIDE, HALF), BF16)],
        yl.reshape(1), q2, s_near, *far, smem=1, flops=256 * NP * HALF,
    )
    s_oth = other(s_out)

    w4 = call(loss_kernel, [sd((4, QDEV, NP), BF16)], s_own, s_oth, count, target)[0]
    w_own = swap(w4, Y)
    w_oth = other(w_own)
    blocks = call(
        pool_kernel, [sd((4, 2 * ROWS, SLICE), F32)],
        jnp.stack([x, y, core]), w_own, w_oth, *group, smem=1,
        scratch=[pltpu.VMEM((1024, NP), BF16), pltpu.VMEM((1024, SLICE), BF16)], flops=2 * 1024 * NP * SLICE,
    )[0]
    sums = call(x_sum_kernel, [sd((16, 48, 128), F32)], swap(blocks, "x"))[0]
    by_z = swap(sums, "z")

    here = 2 * yl + lax.axis_index("yh")
    g_own, g_out = call(
        query_kernel, [sd((QDEV, HALF), F32)] * 2,
        jnp.stack([here, yl]), w_own, w_oth, pool_near, pool_far, sums,
        smem=1, after=1, scratch=[pltpu.VMEM((2 * QDEV, NP), BF16)], flops=2 * 256 * NP * HALF,
    )
    query_grad, token = call(
        join_kernel, [sd((QDEV, D), F32), sd((8, 128), F32)], core.reshape(1), g_own, other(g_out),
        smem=1, out_spaces=(pltpu.HBM, pltpu.VMEM), scratch=[pltpu.SemaphoreType.DMA((2,))],
    )

    by_y = swap(call(z_sum_kernel, [sd((8, 24, 128), F32)], by_z, token, after=1)[0], Y + ("c",))
    passage_grad = call(last_kernel, [sd((6, D), F32)], by_y)[0]
    return query_grad, passage_grad


def solution(mesh):
    fine = Mesh(mesh.devices.reshape(2, 4, 16, 2, 2), ("yl", "x", "z", "yh", "c"))
    every, pooled = ("yl", "x", "z", "yh", "c"), ("yl", "x", "z")
    return jax.shard_map(
        shards,
        mesh=fine,
        in_specs=(P(every, None), P(pooled, None), P(every), P(every, None)),
        out_specs=(P(every, None), P(pooled, None)),
        check_vma=False,
    )
```
